32 devices in a mesh: groups: 2 (over y), ra: 4 (over z), dec: 2 (over x), band: 2 (over core).
Axes of the slice: x: 2, y: 2, z: 4, core: 2. Of those that a mesh axis runs over, the one named last changes fastest.
Arguments:
- sky_maps: bfloat16 [512, 312, 256], P(('groups', 'band'), 'ra', 'dec'), parts along dimension 0, may hold values from -12 to 12
- radii: int32 [512], P(('groups', 'band')), parts along dimension 0, may hold values from 1 to 17, as said below
- valid: int32 [624, 256], P(('groups', 'ra'), 'dec'), parts along dimension 0, may hold values from 0 to 1, as said below
Outputs:
- smoothed: bfloat16 [512, 312, 256], P(('groups', 'band'), 'ra', 'dec'), parts along dimension 0
- channel_mean: float32 [512], P(('groups', 'band')), parts along dimension 0
- covariance: float32 [512, 256], P('groups', 'band'), parts along dimension 0
The draws below stay inside these ranges and needn't reach their ends.
There are 2 independent parts, one for each index of `groups`. The reference program is written for one: setup_inputs(seed, part) draws one part's arguments, and reference() takes and returns one part's arrays. A program takes and returns all parts, laid end to end along the dimension named above; each array names one. Nothing has to cross between parts.
Inputs may be any that keep to these rules, and one draw needn't show every extreme that they name: `radii`: some channel has half-width exactly 17. 1 marks a pixel that enters the statistics; the pixel with declination index 0 is valid in every row.
All inputs are finite; a program needn't handle non-finite values.
Results may differ from the reference program's by a relative error of at most 0.012.
The reference program's roundings to bfloat16 on the way count: a program that leaves them out, or rounds other values in their place, can miss the bound.
Values may be sent and summed in bfloat16 or wider, within the bound.
A program may use at most 64 MiB of HBM per device.

```python
import jax
import jax.numpy as jnp
from jax import lax

CHANNELS = 256
RMAX = 17
NRA = 312
NDEC = 256


def draw_sky_maps(key, part):
    noise_key = jax.random.fold_in(key, 11)
    full_shape = (CHANNELS, NRA, NDEC)
    values = jax.random.normal(noise_key, full_shape, jnp.float32)
    return jnp.clip(values, -12.0, 12.0).astype(jnp.bfloat16)


def draw_radii(key, part):
    pick_key = jax.random.fold_in(key, 21)
    place_key = jax.random.fold_in(key, 22)
    values = jax.random.randint(pick_key, (CHANNELS,), 1, RMAX + 1)
    place = jax.random.randint(place_key, (), 0, CHANNELS)
    return jnp.where(jnp.arange(CHANNELS) == place, RMAX, values).astype(jnp.int32)


def draw_valid(key, part):
    full_shape = (NRA, NDEC)
    along = lax.broadcasted_iota(jnp.int32, full_shape, 0)
    down = lax.broadcasted_iota(jnp.int32, full_shape, 1)
    chance = 200 + 400 * along // NRA + 300 * down // NDEC
    coins = jax.random.randint(jax.random.fold_in(key, 31), full_shape, 0, 1000)
    picked = (coins < chance) | (down == 0)
    return jnp.where(picked, 1, 0).astype(jnp.int32)


def setup_inputs(seed: int = 0, part: int = 0) -> dict:
    seeds = jax.random.split(jax.random.key(seed), 4)
    part_keys = jax.random.split(jax.random.fold_in(seeds[3], part), 4)
    return {
        "sky_maps": draw_sky_maps(jax.random.fold_in(jax.random.fold_in(seeds[3], part), 71), part),
        "radii": draw_radii(jax.random.fold_in(jax.random.fold_in(seeds[3], part), 71), part),
        "valid": draw_valid(jax.random.fold_in(jax.random.fold_in(seeds[3], part), 71), part),
    }


def beam_taps(radii, offsets):
    radius = radii.astype(jnp.float32)
    lead_shape = (radii.shape[0],) + (1,) * offsets.ndim
    radius = radius.reshape(lead_shape)
    spread = 0.5 * radius
    inside = jnp.abs(offsets)[None] <= radius
    return jnp.where(inside, jnp.exp(-(offsets * offsets)[None] / (2.0 * spread * spread)), 0.0)


def reference(sky_maps, radii, valid):
    raw_taps = beam_taps(radii, jnp.arange(-RMAX, RMAX + 1).astype(jnp.float32))
    kernel_taps = (raw_taps / jnp.sum(raw_taps, axis=1)[:, None]).astype(jnp.bfloat16)

    def smooth_one(item):
        plane, weights = item
        values = plane.astype(jnp.float32)
        kernel = weights.astype(jnp.float32)
        padded = jnp.pad(values, ((0, 0), (RMAX, RMAX)))
        across = jnp.zeros(values.shape, jnp.float32)
        for index in range(2 * RMAX + 1):
            across = across + kernel[index] * padded[:, index:index + NDEC]
        across = lax.optimization_barrier(across.astype(jnp.bfloat16)).astype(jnp.float32)
        result = jnp.zeros(values.shape, jnp.float32)
        for index in range(2 * RMAX + 1):
            result = result + kernel[index] * jnp.roll(across, -(index - RMAX), axis=0)
        return result.astype(jnp.bfloat16)

    smoothed = lax.map(smooth_one, (sky_maps, kernel_taps))
    flat = smoothed.reshape(smoothed.shape[0], -1)
    weights = valid.reshape(-1).astype(jnp.float32)
    masked = flat * weights.astype(jnp.bfloat16)[None]
    sums = jnp.sum(masked.astype(jnp.float32), axis=1)
    count = jnp.sum(weights)
    channel_mean = sums / count
    gram = lax.dot_general(masked, masked, (((1,), (1,)), ((), ())), preferred_element_type=jnp.float32)
    covariance = (gram - count * channel_mean[:, None] * channel_mean[None, :]) / (count - 1.0)
    return smoothed, channel_mean, covariance
```

```python
import functools

import jax
import jax.numpy as jnp
from jax import lax
from jax.experimental import pallas as pl
from jax.experimental.pallas import tpu as pltpu
from jax.sharding import PartitionSpec as P

RMAX = 17
WIDE = RMAX + 1
CB = 16
MESH = pl.DeviceIdType.MESH


def up(value, step):
    return -(-value // step) * step


def iota(shape, dim):
    return lax.broadcasted_iota(jnp.int32, shape, dim)


def kernel(
    dims, radii_ref, sky_ref, valid_ref, out_ref, mean_ref, cov_ref,
    tab_dec, tab_ra, xs, hs, os, ps, vb, mine, other,
    pack_up, pack_dn, halo_lo, halo_hi, edge_lo, edge_hi, z_before, z_after,
    acc, shares, total, aux, aux_all,
    s_dec, r_dec, s_ra, r_ra, s_band, r_band, s_rs, r_rs, s_ag, r_ag, s_aux, r_aux,
):
    n_ra, n_dec, rows, chans, cols = dims
    blocks = chans // CB
    rows8 = up(rows, 16)
    groups = cols // WIDE
    per = -(-rows // groups)
    peers = n_ra * n_dec
    reducers = min(peers, chans // 8)
    share = chans // reducers
    ext = 128
    ra, dec, band = lax.axis_index("ra"), lax.axis_index("dec"), lax.axis_index("band")
    rank = ra * n_dec + dec
    nxt, prv = lax.rem(ra + 1, n_ra), lax.rem(ra + n_ra - 1, n_ra)
    twin = {"band": 1 - band}

    def peer_id(p):
        return {"ra": p // n_dec, "dec": lax.rem(p, n_dec)}

    def each_peer(body):
        def step(d, carry):
            body(lax.rem(rank + d, peers))
            return carry
        lax.fori_loop(1, peers, step, 0)

    barrier = pltpu.get_barrier_semaphore()
    each_peer(lambda p: pl.semaphore_signal(barrier, inc=1, device_id=peer_id(p), device_id_type=MESH))
    pl.semaphore_signal(barrier, inc=1, device_id=twin, device_id_type=MESH)
    pl.semaphore_wait(barrier, peers)

    def remote(src, dst, send, recv, target):
        return pltpu.make_async_remote_copy(
            src_ref=src, dst_ref=dst, send_sem=send, recv_sem=recv, device_id=target, device_id_type=MESH
        )

    def dec_up(b):
        return remote(pack_up.at[b], halo_lo.at[b], s_dec.at[0, b], r_dec.at[0, b], {"dec": dec + 1})

    def dec_dn(b):
        return remote(pack_dn.at[b], halo_hi.at[b], s_dec.at[1, b], r_dec.at[1, b], {"dec": dec - 1})

    def ra_up(b):
        return remote(edge_hi.at[b], z_before.at[b], s_ra.at[0, b], r_ra.at[0, b], {"ra": nxt})

    def ra_dn(b):
        return remote(edge_lo.at[b], z_after.at[b], s_ra.at[1, b], r_ra.at[1, b], {"ra": prv})

    def to_twin(b):
        return remote(mine.at[b], other.at[b], s_band.at[b], r_band.at[b], twin)

    has_hi, has_lo = dec < n_dec - 1, dec > 0
    lanes = iota((1, 1, cols), 2)
    tall = per * groups
    xs[...] = jnp.zeros_like(xs)

    def load_block(b):
        at = pl.multiple_of(b * CB, CB)
        block = sky_ref[:, pl.ds(at, CB), :].astype(jnp.float32)
        xs[0:rows * CB, :] = block.reshape(rows * CB, cols)

    def pack_block(b, carry):
        load_block(b)

        def packed(first):
            result = jnp.zeros((per, CB, cols), jnp.float32)
            for g in range(groups):
                part = xs[g * per * CB:(g + 1) * per * CB, :].reshape(per, CB, cols)
                turned = pltpu.roll(part, (WIDE * g - first) % cols, 2)
                inside = (lanes >= WIDE * g) & (lanes < WIDE * (g + 1))
                result = jnp.where(inside, turned, result)
            return result.astype(jnp.bfloat16)

        @pl.when(has_hi)
        def _():
            pack_up[b] = packed(cols - WIDE)
            dec_up(b).start()

        @pl.when(has_lo)
        def _():
            pack_dn[b] = packed(0)
            dec_dn(b).start()

        return carry

    lax.fori_loop(0, blocks, pack_block, 0)

    def table(r, carry):
        radius = r.astype(jnp.float32)
        spread = 0.5 * radius

        def taps(k):
            k = k.astype(jnp.float32)
            return jnp.where(jnp.abs(k) <= radius, jnp.exp(-(k * k) / (2.0 * spread * spread)), 0.0)

        norm = jnp.sum(taps(iota((1, 128), 1) - 64), axis=1, keepdims=True)
        z, y = iota((cols, cols), 0), iota((cols, cols), 1)
        tab_dec[r, 0:cols, :] = (taps(z - y) / norm).astype(jnp.bfloat16)
        j = jnp.where(z < WIDE, cols + z, jnp.where((z >= 64) & (z < 64 + WIDE), z - 64 - WIDE, 4 * cols))
        tab_dec[r, cols:2 * cols, :] = (taps(j - y) / norm).astype(jnp.bfloat16)
        x, e = iota((rows8, ext), 0), iota((rows8, ext), 1)
        at = jnp.where(
            e < rows, e,
            jnp.where(
                (e >= rows8) & (e < rows8 + RMAX), e - rows8 - RMAX,
                jnp.where((e >= rows8 + RMAX) & (e < rows8 + 2 * RMAX), e - rows8 - RMAX + rows, 4 * ext),
            ),
        )
        tab_ra[r] = (taps(at - x) / norm).astype(jnp.bfloat16)
        return carry

    lax.fori_loop(1, RMAX + 1, table, 0)

    used = rows8 + 2 * RMAX

    @pl.when(jnp.logical_not(has_lo))
    def _():
        halo_lo[...] = jnp.zeros_like(halo_lo)

    @pl.when(jnp.logical_not(has_hi))
    def _():
        halo_hi[...] = jnp.zeros_like(halo_hi)

    def dec_block(b, carry):
        load_block(b)
        ps[b, used * CB:ext * CB, :] = jnp.zeros(((ext - used) * CB, cols), jnp.float32)

        @pl.when(has_lo)
        def _():
            dec_up(b).wait_recv()

        @pl.when(has_hi)
        def _():
            dec_dn(b).wait_recv()

        low = halo_lo[b].astype(jnp.float32)
        high = halo_hi[b].astype(jnp.float32)
        for g in range(groups):
            left = pltpu.roll(low, (64 - WIDE * g) % cols, 2)
            right = pltpu.roll(high, (-WIDE * g) % cols, 2)
            both = jnp.where(lanes < 64, right, left)
            hs[g * per * CB:(g + 1) * per * CB, :] = both.reshape(per * CB, cols)
        for c in range(CB):
            rr = radii_ref[b * CB + c]
            main = xs[pl.ds(c, rows8, stride=CB), :]
            side = hs[pl.ds(c, rows8, stride=CB), :]
            left_hand = jnp.concatenate([main, side], axis=1).astype(jnp.bfloat16)
            part = jnp.dot(left_hand, tab_dec[rr], preferred_element_type=jnp.float32)
            part = part.astype(jnp.bfloat16).astype(jnp.float32)
            ps[b, pl.ds(c, rows8, stride=CB), :] = part
        edge_lo[b] = ps[b, 0:RMAX * CB, :].reshape(RMAX, CB, cols).astype(jnp.bfloat16)
        last = ps[b, (rows - RMAX) * CB:rows * CB, :]
        edge_hi[b] = last.reshape(RMAX, CB, cols).astype(jnp.bfloat16)
        ra_up(b).start()
        ra_dn(b).start()
        return carry

    lax.fori_loop(0, blocks, dec_block, 0)

    weights = valid_ref[...].astype(jnp.float32)
    for x in range(rows):
        vb[x] = jnp.broadcast_to(weights[x:x + 1, :], (CB, cols)).astype(jnp.bfloat16)

    def ra_block(b, carry):
        ra_up(b).wait_recv()
        ra_dn(b).wait_recv()
        before = z_before[b].astype(jnp.float32)
        ps[b, rows8 * CB:(rows8 + RMAX) * CB, :] = before.reshape(RMAX * CB, cols)
        after = z_after[b].astype(jnp.float32)
        ps[b, (rows8 + RMAX) * CB:used * CB, :] = after.reshape(RMAX * CB, cols)
        for c in range(CB):
            rr = radii_ref[b * CB + c]
            column = ps[b, pl.ds(c, ext, stride=CB), :].astype(jnp.bfloat16)
            os[pl.ds(c, rows8, stride=CB), :] = jnp.dot(
                tab_ra[rr], column, preferred_element_type=jnp.float32
            )
        smooth = os[0:rows * CB, :].reshape(rows, CB, cols).astype(jnp.bfloat16)
        out_ref[:, pl.ds(pl.multiple_of(b * CB, CB), CB), :] = smooth
        mine[b] = smooth * vb[...]
        to_twin(b).start()
        return carry

    lax.fori_loop(0, blocks, ra_block, 0)

    def twin_wait(b, carry):
        to_twin(b).wait_recv()
        return carry

    lax.fori_loop(0, blocks, twin_wait, 0)

    acc[...] = jnp.zeros_like(acc)
    steps = 6 if rows % 6 == 0 else (2 if rows % 2 == 0 else 1)

    def gram(i, carry):
        def row(ref, x):
            return ref[:, pl.ds(x, 1), :, :].reshape(chans, cols)

        own = jnp.concatenate([row(mine, i * steps + s) for s in range(steps)], axis=1)
        oth = jnp.concatenate([row(other, i * steps + s) for s in range(steps)], axis=1)
        msk = jnp.concatenate([vb[i * steps + s] for s in range(steps)], axis=1)
        acc[...] += lax.dot_general(
            jnp.concatenate([own, msk], axis=0), jnp.concatenate([own, oth], axis=0),
            (((1,), (1,)), ((), ())), preferred_element_type=jnp.float32,
        )
        return carry

    lax.fori_loop(0, rows // steps, gram, 0)

    count = jnp.sum(weights, keepdims=True)
    aux[...] = jnp.where(iota((8, 2 * chans), 0) == 0, acc[chans:chans + 8, :], count)

    def part_of(p):
        return acc.at[pl.ds(pl.multiple_of(p * share, share), share), :]

    def rs(p, slot):
        return remote(part_of(p), shares.at[slot], s_rs.at[p], r_rs.at[slot], peer_id(p))

    def ag(p, slot):
        mypart = total.at[pl.ds(pl.multiple_of(slot * share, share), share), :]
        return remote(mypart, mypart, s_ag.at[p], r_ag.at[slot], peer_id(p))

    def au(p, slot):
        return remote(aux, aux_all.at[slot], s_aux.at[p], r_aux.at[slot], peer_id(p))

    def reducing(p, body):
        if reducers == peers:
            body()
        else:
            pl.when(p < reducers)(body)

    each_peer(lambda p: reducing(p, lambda: rs(p, rank).start()))
    each_peer(lambda p: au(p, rank).start())
    aux_all[rank] = aux[...]

    def reduce_own():
        shares[rank] = acc[pl.ds(pl.multiple_of(rank * share, share), share), :]
        each_peer(lambda p: rs(rank, p).wait_recv())
        whole = shares[0]
        whole = lax.fori_loop(1, peers, lambda p, t: t + shares[p], whole)
        total[pl.ds(pl.multiple_of(rank * share, share), share), :] = whole
        each_peer(lambda p: ag(p, rank).start())

    reducing(rank, reduce_own)
    each_peer(lambda p: au(p, p).wait_recv())
    sums = lax.fori_loop(1, peers, lambda p, t: t + aux_all[p], aux_all[0])
    count = sums[1:2, 0:1]
    means = sums[0:1, :] / count
    mean_ref[...] = means[:, 0:chans]
    column = jnp.transpose(jnp.broadcast_to(means[:, 0:chans], (chans, chans)))
    each_peer(lambda p: reducing(p, lambda: ag(p, p).wait_recv()))
    for k in range(2):
        across = means[:, k * chans:(k + 1) * chans]
        block = (total[:, k * chans:(k + 1) * chans] - count * column * across) / (count - 1.0)
        place = band if k == 0 else 1 - band
        cov_ref[pl.ds(pl.multiple_of(place * chans, chans), chans), :] = jnp.transpose(block)

    def finish(b, carry):
        pl.when(has_hi)(lambda: dec_up(b).wait_send())
        pl.when(has_lo)(lambda: dec_dn(b).wait_send())
        ra_up(b).wait_send()
        ra_dn(b).wait_send()
        to_twin(b).wait_send()
        return carry

    lax.fori_loop(0, blocks, finish, 0)
    each_peer(lambda p: reducing(p, lambda: rs(p, rank).wait_send()))
    each_peer(lambda p: au(p, rank).wait_send())
    reducing(rank, lambda: each_peer(lambda p: ag(p, rank).wait_send()))


def per_device(n_ra, n_dec, sky_maps, radii, valid):
    chans, rows, cols = sky_maps.shape
    blocks = chans // CB
    rows8 = up(rows, 16)
    groups = cols // WIDE
    per = -(-rows // groups)
    peers = n_ra * n_dec
    share = chans // min(peers, chans // 8)
    tall = max(per * groups, rows8)
    f32, b16, dma = jnp.float32, jnp.bfloat16, pltpu.SemaphoreType.DMA
    vmem = pl.BlockSpec(memory_space=pltpu.VMEM)
    flat = jnp.transpose(sky_maps, (1, 0, 2))
    packed = pltpu.VMEM((blocks, per, CB, cols), b16)
    edge = pltpu.VMEM((blocks, RMAX, CB, cols), b16)
    smoothed, mean, cov = pl.pallas_call(
        functools.partial(kernel, (n_ra, n_dec, rows, chans, cols)),
        out_shape=(
            jax.ShapeDtypeStruct((rows, chans, cols), b16),
            jax.ShapeDtypeStruct((1, chans), f32),
            jax.ShapeDtypeStruct((2 * chans, chans), f32),
        ),
        in_specs=[pl.BlockSpec(memory_space=pltpu.SMEM), vmem, vmem],
        out_specs=(vmem, vmem, vmem),
        scratch_shapes=[
            pltpu.VMEM((RMAX + 1, 2 * cols, cols), b16),
            pltpu.VMEM((RMAX + 1, rows8, 128), b16),
            pltpu.VMEM((tall * CB, cols), f32),
            pltpu.VMEM((tall * CB, cols), f32),
            pltpu.VMEM((rows8 * CB, cols), f32),
            pltpu.VMEM((blocks, 128 * CB, cols), f32),
            pltpu.VMEM((rows, CB, cols), b16),
            pltpu.VMEM((blocks, rows, CB, cols), b16),
            pltpu.VMEM((blocks, rows, CB, cols), b16),
            packed, packed, packed, packed,
            edge, edge, edge, edge,
            pltpu.VMEM((chans + CB, 2 * chans), f32),
            pltpu.VMEM((peers, share, 2 * chans), f32),
            pltpu.VMEM((chans, 2 * chans), f32),
            pltpu.VMEM((8, 2 * chans), f32),
            pltpu.VMEM((peers, 8, 2 * chans), f32),
            dma((2, blocks)), dma((2, blocks)), dma((2, blocks)), dma((2, blocks)),
            dma((blocks,)), dma((blocks,)),
            dma((peers,)), dma((peers,)), dma((peers,)), dma((peers,)), dma((peers,)), dma((peers,)),
        ],
        compiler_params=pltpu.CompilerParams(
            collective_id=0, has_side_effects=True, vmem_limit_bytes=52 * 1024 * 1024
        ),
    )(radii, flat, valid)
    return (jnp.transpose(smoothed, (1, 0, 2)), mean.reshape(chans), cov)


def solution(mesh):
    return jax.shard_map(
        functools.partial(per_device, mesh.shape["ra"], mesh.shape["dec"]),
        mesh=mesh,
        in_specs=(
            P(("groups", "band"), "ra", "dec"),
            P(("groups", "band")),
            P(("groups", "ra"), "dec"),
        ),
        out_specs=(P(("groups", "band"), "ra", "dec"), P(("groups", "band")), P("groups", "band")),
        check_vma=False,
    )
```

```python
import functools

import jax
import jax.numpy as jnp
from jax import lax
from jax.experimental import pallas as pl
from jax.experimental.pallas import tpu as pltpu
from jax.sharding import PartitionSpec as P

RMAX = 17
WIDE = RMAX + 1
CB = 16
MESH = pl.DeviceIdType.MESH


def up(value, step):
    return -(-value // step) * step


def iota(shape, dim):
    return lax.broadcasted_iota(jnp.int32, shape, dim)


def inner_rows(rows):
    first = RMAX // 16 * 16
    last = up(rows - RMAX, 16)
    return first, last - first, up(RMAX, 8)


def kernel(
    dims, radii_ref, sky_hbm, valid_hbm, out_ref, mean_ref, cov_ref,
    sky_ref, valid_ref, loads,
    tab_dec, tab_in, tab_ed, xs, hs, os, ps, vb, mine_in, mine_ed, other_in, other_ed,
    pack_up, pack_dn, halo_lo, halo_hi, edge_lo, edge_hi, z_before, z_after,
    acc, shares, total, aux, aux_all,
    s_dec, r_dec, s_ra, r_ra, s_band, r_band, s_rs, r_rs, s_ag, r_ag, s_aux, r_aux,
):
    n_ra, n_dec, rows, chans, cols = dims
    blocks = chans // CB
    rows8 = up(rows, 16)
    groups = cols // WIDE
    per = -(-rows // groups)
    peers = n_ra * n_dec
    reducers = min(peers, chans // 8)
    share = chans // reducers
    ext = 128
    in_at, in_rows, edge_rows = inner_rows(rows)
    ra, dec, band = lax.axis_index("ra"), lax.axis_index("dec"), lax.axis_index("band")
    rank = ra * n_dec + dec
    nxt, prv = lax.rem(ra + 1, n_ra), lax.rem(ra + n_ra - 1, n_ra)
    twin = {"band": 1 - band}

    def peer_id(p):
        return {"ra": p // n_dec, "dec": lax.rem(p, n_dec)}

    def each_peer(body):
        def step(d, carry):
            body(lax.rem(rank + d, peers))
            return carry
        lax.fori_loop(1, peers, step, 0)

    def table(r, carry):
        radius = r.astype(jnp.float32)
        spread = 0.5 * radius
        k = lax.rem(iota((8, cols), 0) - iota((8, cols), 1) + cols + cols // 2, cols) - cols // 2
        k = k.astype(jnp.float32)
        raw = jnp.where(jnp.abs(k) <= radius, jnp.exp(-(k * k) / (2.0 * spread * spread)), 0.0)
        first = raw / jnp.sum(raw, axis=1, keepdims=True)
        full = jnp.concatenate([pltpu.roll(first, 8 * t, 1) for t in range(cols // 8)], axis=0)
        near = jnp.abs(iota((cols, cols), 0) - iota((cols, cols), 1)) <= cols // 2
        tab_in[r] = full[in_at:in_at + in_rows].astype(jnp.bfloat16)
        ends = jnp.concatenate([full[0:edge_rows], full[rows8 - edge_rows:rows8]], axis=0)
        tab_ed[r] = ends.astype(jnp.bfloat16)
        tab_dec[r, 0:cols, :] = jnp.where(near, full, 0.0).astype(jnp.bfloat16)
        tab_dec[r, cols:2 * cols, :] = jnp.where(near, 0.0, full).astype(jnp.bfloat16)
        return carry

    load_sky = pltpu.make_async_copy(sky_hbm, sky_ref, loads.at[0])
    load_valid = pltpu.make_async_copy(valid_hbm, valid_ref, loads.at[1])
    load_sky.start()
    load_valid.start()
    barrier = pltpu.get_barrier_semaphore()
    each_peer(lambda p: pl.semaphore_signal(barrier, inc=1, device_id=peer_id(p), device_id_type=MESH))
    pl.semaphore_signal(barrier, inc=1, device_id=twin, device_id_type=MESH)
    lax.fori_loop(1, RMAX + 1, table, 0)
    load_sky.wait()
    pl.semaphore_wait(barrier, peers)

    def remote(src, dst, send, recv, target):
        return pltpu.make_async_remote_copy(
            src_ref=src, dst_ref=dst, send_sem=send, recv_sem=recv, device_id=target, device_id_type=MESH
        )

    def dec_up(b):
        return remote(pack_up.at[b], halo_lo.at[b], s_dec.at[0, b], r_dec.at[0, b], {"dec": dec + 1})

    def dec_dn(b):
        return remote(pack_dn.at[b], halo_hi.at[b], s_dec.at[1, b], r_dec.at[1, b], {"dec": dec - 1})

    def ra_up(b):
        return remote(edge_hi.at[b], z_before.at[b], s_ra.at[0, b], r_ra.at[0, b], {"ra": nxt})

    def ra_dn(b):
        return remote(edge_lo.at[b], z_after.at[b], s_ra.at[1, b], r_ra.at[1, b], {"ra": prv})

    def to_twin(k, b):
        mine, other = ((mine_ed, other_ed), (mine_in, other_in))[k]
        return remote(mine.at[b], other.at[b], s_band.at[k, b], r_band.at[k, b], twin)

    has_hi, has_lo = dec < n_dec - 1, dec > 0
    lanes = iota((1, 1, cols), 2)
    inner = rows - 2 * RMAX
    order = [*range(RMAX), *range(rows - RMAX, rows), *range(RMAX, rows - RMAX)]
    tall = per * groups
    xs[...] = jnp.zeros_like(xs)
    hs[...] = jnp.zeros_like(hs)

    def load_block(b):
        at = pl.multiple_of(b * CB, CB)
        block = sky_ref[:, pl.ds(at, CB), :].astype(jnp.float32)
        xs[0:rows * CB, :] = block.reshape(rows * CB, cols)

    def pack_block(b):
        at = pl.multiple_of(b * CB, CB)

        def packed(first):
            result = jnp.zeros((per, CB, cols), jnp.float32)
            for g in range(groups):
                end = min(rows, (g + 1) * per)
                part = sky_ref[g * per:end, pl.ds(at, CB), :].astype(jnp.float32)
                if end < (g + 1) * per:
                    fill = jnp.zeros(((g + 1) * per - end, CB, cols), jnp.float32)
                    part = jnp.concatenate([part, fill], axis=0)
                turned = pltpu.roll(part, (WIDE * g - first) % cols, 2)
                inside = (lanes >= WIDE * g) & (lanes < WIDE * (g + 1))
                result = jnp.where(inside, turned, result)
            return result.astype(jnp.bfloat16)

        @pl.when(has_hi)
        def _():
            pack_up[b] = packed(cols - WIDE)
            dec_up(b).start()

        @pl.when(has_lo)
        def _():
            pack_dn[b] = packed(0)
            dec_dn(b).start()

    ahead = min(2, blocks)
    for b in range(ahead):
        pack_block(jnp.int32(b))

    load_valid.wait()
    weights = valid_ref[...].astype(jnp.float32)
    for at, x in enumerate(order):
        vb[at] = jnp.broadcast_to(weights[x:x + 1, :], (CB, cols)).astype(jnp.bfloat16)

    def unpack(b, side):
        low = None if side == "high" else halo_lo[b].astype(jnp.float32)
        high = None if side == "low" else halo_hi[b].astype(jnp.float32)
        for g in range(groups):
            if side != "high":
                left = pltpu.roll(low, (cols - WIDE - WIDE * g) % cols, 2)
            if side != "low":
                right = pltpu.roll(high, (-WIDE * g) % cols, 2)
            on_right = lanes < cols // 2
            if side == "both":
                both = jnp.where(on_right, right, left)
            elif side == "low":
                both = jnp.where(on_right, 0.0, left)
            else:
                both = jnp.where(on_right, right, 0.0)
            hs[g * per * CB:(g + 1) * per * CB, :] = both.reshape(per * CB, cols)

    def for_blocks(body):
        def step(b, carry):
            body(b)
            return carry
        lax.fori_loop(0, blocks, step, 0)

    def smooth_rows(b, tab, height):
        for c in range(CB):
            rr = radii_ref[b * CB + c]
            column = ps[b, pl.ds(c, ext, stride=CB), :].astype(jnp.bfloat16)
            os[pl.ds(c, height, stride=CB), :] = jnp.dot(
                tab[rr], column, preferred_element_type=jnp.float32
            )

    def gram_of(mine, other, first, height):
        steps = next(n for n in (8, 6, 4, 2, 1) if height % n == 0)
        if height % 34 == 0:
            steps = 34
        if height % 22 == 0:
            steps = 22

        def gram(i, carry):
            def row(ref, x):
                return ref[:, pl.ds(x, 1), :, :].reshape(chans, cols)

            own = jnp.concatenate([row(mine, i * steps + s) for s in range(steps)], axis=1)
            oth = jnp.concatenate([row(other, i * steps + s) for s in range(steps)], axis=1)
            msk = jnp.concatenate([vb[first + i * steps + s] for s in range(steps)], axis=1)
            acc[...] += lax.dot_general(
                jnp.concatenate([own, msk], axis=0), jnp.concatenate([own, oth], axis=0),
                (((1,), (1,)), ((), ())), preferred_element_type=jnp.float32,
            )
            return carry

        lax.fori_loop(0, height // steps, gram, 0)

    def dec_block(b, carry):
        @pl.when(b + ahead < blocks)
        def _():
            pack_block(b + ahead)

        load_block(b)
        ps[b, rows8 * CB:ext * CB, :] = jnp.zeros(((ext - rows8) * CB, cols), jnp.float32)

        @pl.when(has_lo)
        def _():
            dec_up(b).wait_recv()

        @pl.when(has_hi)
        def _():
            dec_dn(b).wait_recv()

        @pl.when(has_lo & has_hi)
        def _():
            unpack(b, "both")

        @pl.when(has_lo & jnp.logical_not(has_hi))
        def _():
            unpack(b, "low")

        @pl.when(has_hi & jnp.logical_not(has_lo))
        def _():
            unpack(b, "high")

        for c in range(CB):
            rr = radii_ref[b * CB + c]
            main = xs[pl.ds(c, rows8, stride=CB), :]
            side = hs[pl.ds(c, rows8, stride=CB), :]
            left_hand = jnp.concatenate([main, side], axis=1).astype(jnp.bfloat16)
            part = jnp.dot(left_hand, tab_dec[rr], preferred_element_type=jnp.float32)
            part = part.astype(jnp.bfloat16).astype(jnp.float32)
            ps[b, pl.ds(c, rows8, stride=CB), :] = part
        edge_lo[b] = ps[b, 0:RMAX * CB, :].reshape(RMAX, CB, cols).astype(jnp.bfloat16)
        last = ps[b, (rows - RMAX) * CB:rows * CB, :]
        edge_hi[b] = last.reshape(RMAX, CB, cols).astype(jnp.bfloat16)
        ra_up(b).start()
        ra_dn(b).start()
        smooth_rows(b, tab_in, in_rows)
        at = RMAX - in_at
        smooth = os[at * CB:(at + inner) * CB, :].reshape(inner, CB, cols).astype(jnp.bfloat16)
        out_ref[RMAX:rows - RMAX, pl.ds(pl.multiple_of(b * CB, CB), CB), :] = smooth
        mine_in[b] = smooth * vb[2 * RMAX:rows]
        to_twin(1, b).start()
        return carry

    lax.fori_loop(0, blocks, dec_block, 0)
    for_blocks(lambda b: to_twin(1, b).wait_recv())
    acc[...] = jnp.zeros_like(acc)
    gram_of(mine_in, other_in, 2 * RMAX, inner)

    def ra_block(b, carry):
        ra_up(b).wait_recv()
        ra_dn(b).wait_recv()
        before = z_before[b].astype(jnp.float32)
        ps[b, (ext - RMAX) * CB:ext * CB, :] = before.reshape(RMAX * CB, cols)
        after = z_after[b].astype(jnp.float32)
        ps[b, rows * CB:(rows + RMAX) * CB, :] = after.reshape(RMAX * CB, cols)
        smooth_rows(b, tab_ed, 2 * edge_rows)
        low = os[0:RMAX * CB, :].reshape(RMAX, CB, cols).astype(jnp.bfloat16)
        at = 2 * edge_rows - rows8 + rows - RMAX
        high = os[at * CB:(at + RMAX) * CB, :].reshape(RMAX, CB, cols).astype(jnp.bfloat16)
        here = pl.ds(pl.multiple_of(b * CB, CB), CB)
        out_ref[0:RMAX, here, :] = low
        out_ref[rows - RMAX:rows, here, :] = high
        mine_ed[b, 0:RMAX] = low * vb[0:RMAX]
        mine_ed[b, RMAX:2 * RMAX] = high * vb[RMAX:2 * RMAX]
        to_twin(0, b).start()
        return carry

    lax.fori_loop(0, blocks, ra_block, 0)
    for_blocks(lambda b: to_twin(0, b).wait_recv())
    gram_of(mine_ed, other_ed, 0, 2 * RMAX)
    count = jnp.sum(weights, keepdims=True)
    aux[...] = jnp.where(iota((8, 2 * chans), 0) == 0, acc[chans:chans + 8, :], count)

    def part_of(p):
        return acc.at[pl.ds(pl.multiple_of(p * share, share), share), :]

    def rs(p, slot):
        return remote(part_of(p), shares.at[slot], s_rs.at[p], r_rs.at[slot], peer_id(p))

    def ag(p, slot):
        mypart = total.at[pl.ds(pl.multiple_of(slot * share, share), share), :]
        return remote(mypart, mypart, s_ag.at[p], r_ag.at[slot], peer_id(p))

    def au(p, slot):
        return remote(aux, aux_all.at[slot], s_aux.at[p], r_aux.at[slot], peer_id(p))

    def reducing(p, body):
        if reducers == peers:
            body()
        else:
            pl.when(p < reducers)(body)

    each_peer(lambda p: reducing(p, lambda: rs(p, rank).start()))
    each_peer(lambda p: au(p, rank).start())
    aux_all[rank] = aux[...]

    def reduce_own():
        shares[rank] = acc[pl.ds(pl.multiple_of(rank * share, share), share), :]
        each_peer(lambda p: rs(rank, p).wait_recv())
        whole = shares[0]
        whole = lax.fori_loop(1, peers, lambda p, t: t + shares[p], whole)
        total[pl.ds(pl.multiple_of(rank * share, share), share), :] = whole
        each_peer(lambda p: ag(p, rank).start())

    reducing(rank, reduce_own)
    each_peer(lambda p: au(p, p).wait_recv())
    sums = lax.fori_loop(1, peers, lambda p, t: t + aux_all[p], aux_all[0])
    count = sums[1:2, 0:1]
    means = sums[0:1, :] / count
    mean_ref[...] = means[:, 0:chans]
    column = jnp.transpose(jnp.broadcast_to(means[:, 0:chans], (chans, chans)))
    each_peer(lambda p: reducing(p, lambda: ag(p, p).wait_recv()))
    for k in range(2):
        across = means[:, k * chans:(k + 1) * chans]
        block = (total[:, k * chans:(k + 1) * chans] - count * column * across) / (count - 1.0)
        place = band if k == 0 else 1 - band
        cov_ref[pl.ds(pl.multiple_of(place * chans, chans), chans), :] = jnp.transpose(block)

    def finish(b, carry):
        pl.when(has_hi)(lambda: dec_up(b).wait_send())
        pl.when(has_lo)(lambda: dec_dn(b).wait_send())
        ra_up(b).wait_send()
        ra_dn(b).wait_send()
        to_twin(0, b).wait_send()
        to_twin(1, b).wait_send()
        return carry

    lax.fori_loop(0, blocks, finish, 0)
    each_peer(lambda p: reducing(p, lambda: rs(p, rank).wait_send()))
    each_peer(lambda p: au(p, rank).wait_send())
    reducing(rank, lambda: each_peer(lambda p: ag(p, rank).wait_send()))


def per_device(n_ra, n_dec, sky_maps, radii, valid):
    chans, rows, cols = sky_maps.shape
    blocks = chans // CB
    rows8 = up(rows, 16)
    groups = cols // WIDE
    per = -(-rows // groups)
    peers = n_ra * n_dec
    share = chans // min(peers, chans // 8)
    tall = max(per * groups, rows8)
    f32, b16, dma = jnp.float32, jnp.bfloat16, pltpu.SemaphoreType.DMA
    vmem = pl.BlockSpec(memory_space=pltpu.VMEM)
    hbm = pl.BlockSpec(memory_space=pltpu.HBM)
    in_at, in_rows, edge_rows = inner_rows(rows)
    inner, outer = rows - 2 * RMAX, 2 * RMAX
    flat = jnp.transpose(sky_maps, (1, 0, 2))
    packed = pltpu.VMEM((blocks, per, CB, cols), b16)
    edge = pltpu.VMEM((blocks, RMAX, CB, cols), b16)
    smoothed, mean, cov = pl.pallas_call(
        functools.partial(kernel, (n_ra, n_dec, rows, chans, cols)),
        out_shape=(
            jax.ShapeDtypeStruct((rows, chans, cols), b16),
            jax.ShapeDtypeStruct((1, chans), f32),
            jax.ShapeDtypeStruct((2 * chans, chans), f32),
        ),
        in_specs=[pl.BlockSpec(memory_space=pltpu.SMEM), hbm, hbm],
        out_specs=(vmem, vmem, vmem),
        scratch_shapes=[
            pltpu.VMEM((rows, chans, cols), b16),
            pltpu.VMEM((rows, cols), jnp.int32),
            dma((2,)),
            pltpu.VMEM((RMAX + 1, 2 * cols, cols), b16),
            pltpu.VMEM((RMAX + 1, in_rows, 128), b16),
            pltpu.VMEM((RMAX + 1, 2 * edge_rows, 128), b16),
            pltpu.VMEM((tall * CB, cols), f32),
            pltpu.VMEM((tall * CB, cols), f32),
            pltpu.VMEM((rows8 * CB, cols), f32),
            pltpu.VMEM((blocks, 128 * CB, cols), f32),
            pltpu.VMEM((rows, CB, cols), b16),
            pltpu.VMEM((blocks, inner, CB, cols), b16),
            pltpu.VMEM((blocks, outer, CB, cols), b16),
            pltpu.VMEM((blocks, inner, CB, cols), b16),
            pltpu.VMEM((blocks, outer, CB, cols), b16),
            packed, packed, packed, packed,
            edge, edge, edge, edge,
            pltpu.VMEM((chans + CB, 2 * chans), f32),
            pltpu.VMEM((peers, share, 2 * chans), f32),
            pltpu.VMEM((chans, 2 * chans), f32),
            pltpu.VMEM((8, 2 * chans), f32),
            pltpu.VMEM((peers, 8, 2 * chans), f32),
            dma((2, blocks)), dma((2, blocks)), dma((2, blocks)), dma((2, blocks)),
            dma((2, blocks)), dma((2, blocks)),
            dma((peers,)), dma((peers,)), dma((peers,)), dma((peers,)), dma((peers,)), dma((peers,)),
        ],
        compiler_params=pltpu.CompilerParams(
            collective_id=0, has_side_effects=True, vmem_limit_bytes=32 * 1024 * 1024
        ),
    )(radii, flat, valid)
    return (jnp.transpose(smoothed, (1, 0, 2)), mean.reshape(chans), cov)


def solution(mesh):
    return jax.shard_map(
        functools.partial(per_device, mesh.shape["ra"], mesh.shape["dec"]),
        mesh=mesh,
        in_specs=(
            P(("groups", "band"), "ra", "dec"),
            P(("groups", "band")),
            P(("groups", "ra"), "dec"),
        ),
        out_specs=(P(("groups", "band"), "ra", "dec"), P(("groups", "band")), P("groups", "band")),
        check_vma=False,
    )
```

```python
import functools

import jax
import jax.numpy as jnp
from jax import lax
from jax.experimental import pallas as pl
from jax.experimental.pallas import tpu as pltpu
from jax.sharding import PartitionSpec as P

RMAX = 17
WIDE = RMAX + 1
CB = 16
MESH = pl.DeviceIdType.MESH


def up(value, step):
    return -(-value // step) * step


def iota(shape, dim):
    return lax.broadcasted_iota(jnp.int32, shape, dim)


def inner_rows(rows):
    first = RMAX // 16 * 16
    last = up(rows - RMAX, 16)
    return first, last - first, up(RMAX, 8)


def kernel(
    dims, radii_ref, sky_hbm, valid_hbm, out_ref, mean_ref, cov_ref,
    sky_ref, valid_ref, loads,
    tab_dec, tab_in, tab_ed, xs, hs, os, ps, vb, mine_in, mine_ed, other_in, other_ed,
    pack_up, pack_dn, halo_lo, halo_hi, edge_lo, edge_hi, z_before, z_after,
    acc, shares, total, aux, aux_all,
    s_dec, r_dec, s_ra, r_ra, s_band, r_band, s_rs, r_rs, s_ag, r_ag, s_aux, r_aux,
):
    n_ra, n_dec, rows, chans, cols = dims
    blocks = chans // CB
    rows8 = up(rows, 16)
    groups = cols // WIDE
    per = -(-rows // groups)
    peers = n_ra * n_dec
    reducers = min(peers, chans // 8)
    share = chans // reducers
    ext = 128
    in_at, in_rows, edge_rows = inner_rows(rows)
    ra, dec, band = lax.axis_index("ra"), lax.axis_index("dec"), lax.axis_index("band")
    rank = ra * n_dec + dec
    nxt, prv = lax.rem(ra + 1, n_ra), lax.rem(ra + n_ra - 1, n_ra)
    twin = {"band": 1 - band}

    def peer_id(p):
        return {"ra": p // n_dec, "dec": lax.rem(p, n_dec)}

    def each_peer(body):
        def step(d, carry):
            body(lax.rem(rank + d, peers))
            return carry
        lax.fori_loop(1, peers, step, 0)

    def table(r, carry):
        radius = r.astype(jnp.float32)
        spread = 0.5 * radius
        k = lax.rem(iota((8, cols), 0) - iota((8, cols), 1) + cols + cols // 2, cols) - cols // 2
        k = k.astype(jnp.float32)
        raw = jnp.where(jnp.abs(k) <= radius, jnp.exp(-(k * k) / (2.0 * spread * spread)), 0.0)
        first = raw / jnp.sum(raw, axis=1, keepdims=True)
        full = jnp.concatenate([pltpu.roll(first, 8 * t, 1) for t in range(cols // 8)], axis=0)
        near = jnp.abs(iota((cols, cols), 0) - iota((cols, cols), 1)) <= cols // 2
        tab_in[r] = full[in_at:in_at + in_rows].astype(jnp.bfloat16)
        ends = jnp.concatenate([full[0:edge_rows], full[rows8 - edge_rows:rows8]], axis=0)
        tab_ed[r] = ends.astype(jnp.bfloat16)
        tab_dec[r, 0:cols, :] = jnp.where(near, full, 0.0).astype(jnp.bfloat16)
        tab_dec[r, cols:2 * cols, :] = jnp.where(near, 0.0, full).astype(jnp.bfloat16)
        return carry

    load_sky = pltpu.make_async_copy(sky_hbm, sky_ref, loads.at[0])
    load_valid = pltpu.make_async_copy(valid_hbm, valid_ref, loads.at[1])
    load_sky.start()
    load_valid.start()
    barrier = pltpu.get_barrier_semaphore()
    each_peer(lambda p: pl.semaphore_signal(barrier, inc=1, device_id=peer_id(p), device_id_type=MESH))
    pl.semaphore_signal(barrier, inc=1, device_id=twin, device_id_type=MESH)
    lax.fori_loop(1, RMAX + 1, table, 0)
    load_sky.wait()
    pl.semaphore_wait(barrier, peers)

    def remote(src, dst, send, recv, target):
        return pltpu.make_async_remote_copy(
            src_ref=src, dst_ref=dst, send_sem=send, recv_sem=recv, device_id=target, device_id_type=MESH
        )

    def dec_up(b):
        return remote(pack_up.at[b], halo_lo.at[b], s_dec.at[0, b], r_dec.at[0, b], {"dec": dec + 1})

    def dec_dn(b):
        return remote(pack_dn.at[b], halo_hi.at[b], s_dec.at[1, b], r_dec.at[1, b], {"dec": dec - 1})

    def ra_up(b):
        return remote(edge_hi.at[b], z_before.at[b], s_ra.at[0, b], r_ra.at[0, b], {"ra": nxt})

    def ra_dn(b):
        return remote(edge_lo.at[b], z_after.at[b], s_ra.at[1, b], r_ra.at[1, b], {"ra": prv})

    def to_twin(k, b):
        mine, other = ((mine_ed, other_ed), (mine_in, other_in))[k]
        return remote(mine.at[b], other.at[b], s_band.at[k, b], r_band.at[k, b], twin)

    has_hi, has_lo = dec < n_dec - 1, dec > 0
    lanes = iota((1, 1, cols), 2)
    inner = rows - 2 * RMAX
    order = [*range(RMAX), *range(rows - RMAX, rows), *range(RMAX, rows - RMAX)]
    tall = per * groups
    xs[...] = jnp.zeros_like(xs)
    hs[...] = jnp.zeros_like(hs)

    def load_block(b):
        at = pl.multiple_of(b * CB, CB)
        block = sky_ref[:, pl.ds(at, CB), :].astype(jnp.float32)
        xs[0:rows * CB, :] = block.reshape(rows * CB, cols)

    def pack_block(b):
        at = pl.multiple_of(b * CB, CB)

        def packed(first):
            result = jnp.zeros((per, CB, cols), jnp.float32)
            for g in range(groups):
                end = min(rows, (g + 1) * per)
                part = sky_ref[g * per:end, pl.ds(at, CB), :].astype(jnp.float32)
                if end < (g + 1) * per:
                    fill = jnp.zeros(((g + 1) * per - end, CB, cols), jnp.float32)
                    part = jnp.concatenate([part, fill], axis=0)
                turned = pltpu.roll(part, (WIDE * g - first) % cols, 2)
                inside = (lanes >= WIDE * g) & (lanes < WIDE * (g + 1))
                result = jnp.where(inside, turned, result)
            return result.astype(jnp.bfloat16)

        @pl.when(has_hi)
        def _():
            pack_up[b] = packed(cols - WIDE)
            dec_up(b).start()

        @pl.when(has_lo)
        def _():
            pack_dn[b] = packed(0)
            dec_dn(b).start()

    ahead = min(2, blocks)
    for b in range(ahead):
        pack_block(jnp.int32(b))

    load_valid.wait()
    weights = valid_ref[...].astype(jnp.float32)
    for at, x in enumerate(order):
        vb[at] = jnp.broadcast_to(weights[x:x + 1, :], (CB, cols)).astype(jnp.bfloat16)

    def unpack(b, side):
        low = None if side == "high" else halo_lo[b].astype(jnp.float32)
        high = None if side == "low" else halo_hi[b].astype(jnp.float32)
        for g in range(groups):
            if side != "high":
                left = pltpu.roll(low, (cols - WIDE - WIDE * g) % cols, 2)
            if side != "low":
                right = pltpu.roll(high, (-WIDE * g) % cols, 2)
            on_right = lanes < cols // 2
            if side == "both":
                both = jnp.where(on_right, right, left)
            elif side == "low":
                both = jnp.where(on_right, 0.0, left)
            else:
                both = jnp.where(on_right, right, 0.0)
            hs[g * per * CB:(g + 1) * per * CB, :] = both.reshape(per * CB, cols)

    def for_blocks(body):
        def step(b, carry):
            body(b)
            return carry
        lax.fori_loop(0, blocks, step, 0)

    def smooth_rows(b, tab, height):
        for c in range(CB):
            rr = radii_ref[b * CB + c]
            column = ps[b, pl.ds(c, ext, stride=CB), :].astype(jnp.bfloat16)
            os[pl.ds(c, height, stride=CB), :] = jnp.dot(
                tab[rr], column, preferred_element_type=jnp.float32
            )

    def gram_of(mine, other, first, height):
        steps = next(n for n in (8, 6, 4, 2, 1) if height % n == 0)
        if height % 34 == 0:
            steps = 34
        if height % 22 == 0:
            steps = 22

        def gram(i, carry):
            def row(ref, x):
                return ref[:, pl.ds(x, 1), :, :].reshape(chans, cols)

            own = jnp.concatenate([row(mine, i * steps + s) for s in range(steps)], axis=1)
            oth = jnp.concatenate([row(other, i * steps + s) for s in range(steps)], axis=1)
            msk = jnp.concatenate([vb[first + i * steps + s] for s in range(steps)], axis=1)
            acc[...] += lax.dot_general(
                jnp.concatenate([own, msk], axis=0), jnp.concatenate([own, oth], axis=0),
                (((1,), (1,)), ((), ())), preferred_element_type=jnp.float32,
            )
            return carry

        lax.fori_loop(0, height // steps, gram, 0)

    def dec_block(b, carry):
        @pl.when(b + ahead < blocks)
        def _():
            pack_block(b + ahead)

        load_block(b)
        ps[b, rows8 * CB:ext * CB, :] = jnp.zeros(((ext - rows8) * CB, cols), jnp.float32)

        @pl.when(has_lo)
        def _():
            dec_up(b).wait_recv()

        @pl.when(has_hi)
        def _():
            dec_dn(b).wait_recv()

        @pl.when(has_lo & has_hi)
        def _():
            unpack(b, "both")

        @pl.when(has_lo & jnp.logical_not(has_hi))
        def _():
            unpack(b, "low")

        @pl.when(has_hi & jnp.logical_not(has_lo))
        def _():
            unpack(b, "high")

        for c in range(CB):
            rr = radii_ref[b * CB + c]
            main = xs[pl.ds(c, rows8, stride=CB), :]
            side = hs[pl.ds(c, rows8, stride=CB), :]
            left_hand = jnp.concatenate([main, side], axis=1).astype(jnp.bfloat16)
            part = jnp.dot(left_hand, tab_dec[rr], preferred_element_type=jnp.float32)
            part = part.astype(jnp.bfloat16).astype(jnp.float32)
            ps[b, pl.ds(c, rows8, stride=CB), :] = part
        edge_lo[b] = ps[b, 0:RMAX * CB, :].reshape(RMAX, CB, cols).astype(jnp.bfloat16)
        last = ps[b, (rows - RMAX) * CB:rows * CB, :]
        edge_hi[b] = last.reshape(RMAX, CB, cols).astype(jnp.bfloat16)
        ra_up(b).start()
        ra_dn(b).start()
        return carry

    def inner_block(b):
        smooth_rows(b, tab_in, in_rows)
        at = RMAX - in_at
        smooth = os[at * CB:(at + inner) * CB, :].reshape(inner, CB, cols).astype(jnp.bfloat16)
        out_ref[RMAX:rows - RMAX, pl.ds(pl.multiple_of(b * CB, CB), CB), :] = smooth
        mine_in[b] = smooth * vb[2 * RMAX:rows]
        to_twin(1, b).start()

    lax.fori_loop(0, blocks, dec_block, 0)
    for_blocks(inner_block)
    for_blocks(lambda b: to_twin(1, b).wait_recv())
    acc[...] = jnp.zeros_like(acc)
    gram_of(mine_in, other_in, 2 * RMAX, inner)

    def ra_block(b, carry):
        ra_up(b).wait_recv()
        ra_dn(b).wait_recv()
        before = z_before[b].astype(jnp.float32)
        ps[b, (ext - RMAX) * CB:ext * CB, :] = before.reshape(RMAX * CB, cols)
        after = z_after[b].astype(jnp.float32)
        ps[b, rows * CB:(rows + RMAX) * CB, :] = after.reshape(RMAX * CB, cols)
        smooth_rows(b, tab_ed, 2 * edge_rows)
        low = os[0:RMAX * CB, :].reshape(RMAX, CB, cols).astype(jnp.bfloat16)
        at = 2 * edge_rows - rows8 + rows - RMAX
        high = os[at * CB:(at + RMAX) * CB, :].reshape(RMAX, CB, cols).astype(jnp.bfloat16)
        here = pl.ds(pl.multiple_of(b * CB, CB), CB)
        out_ref[0:RMAX, here, :] = low
        out_ref[rows - RMAX:rows, here, :] = high
        mine_ed[b, 0:RMAX] = low * vb[0:RMAX]
        mine_ed[b, RMAX:2 * RMAX] = high * vb[RMAX:2 * RMAX]
        to_twin(0, b).start()
        return carry

    lax.fori_loop(0, blocks, ra_block, 0)
    for_blocks(lambda b: to_twin(0, b).wait_recv())
    gram_of(mine_ed, other_ed, 0, 2 * RMAX)
    count = jnp.sum(weights, keepdims=True)
    aux[...] = jnp.where(iota((8, 2 * chans), 0) == 0, acc[chans:chans + 8, :], count)

    def part_of(p):
        return acc.at[pl.ds(pl.multiple_of(p * share, share), share), :]

    def rs(p, slot):
        return remote(part_of(p), shares.at[slot], s_rs.at[p], r_rs.at[slot], peer_id(p))

    def ag(p, slot):
        mypart = total.at[pl.ds(pl.multiple_of(slot * share, share), share), :]
        return remote(mypart, mypart, s_ag.at[p], r_ag.at[slot], peer_id(p))

    def au(p, slot):
        return remote(aux, aux_all.at[slot], s_aux.at[p], r_aux.at[slot], peer_id(p))

    def reducing(p, body):
        if reducers == peers:
            body()
        else:
            pl.when(p < reducers)(body)

    each_peer(lambda p: reducing(p, lambda: rs(p, rank).start()))
    each_peer(lambda p: au(p, rank).start())
    aux_all[rank] = aux[...]

    def reduce_own():
        shares[rank] = acc[pl.ds(pl.multiple_of(rank * share, share), share), :]
        each_peer(lambda p: rs(rank, p).wait_recv())
        whole = shares[0]
        whole = lax.fori_loop(1, peers, lambda p, t: t + shares[p], whole)
        total[pl.ds(pl.multiple_of(rank * share, share), share), :] = whole
        each_peer(lambda p: ag(p, rank).start())

    reducing(rank, reduce_own)
    each_peer(lambda p: au(p, p).wait_recv())
    sums = lax.fori_loop(1, peers, lambda p, t: t + aux_all[p], aux_all[0])
    count = sums[1:2, 0:1]
    means = sums[0:1, :] / count
    mean_ref[...] = means[:, 0:chans]
    column = jnp.transpose(jnp.broadcast_to(means[:, 0:chans], (chans, chans)))
    each_peer(lambda p: reducing(p, lambda: ag(p, p).wait_recv()))
    for k in range(2):
        across = means[:, k * chans:(k + 1) * chans]
        block = (total[:, k * chans:(k + 1) * chans] - count * column * across) / (count - 1.0)
        place = band if k == 0 else 1 - band
        cov_ref[pl.ds(pl.multiple_of(place * chans, chans), chans), :] = jnp.transpose(block)

    def finish(b, carry):
        pl.when(has_hi)(lambda: dec_up(b).wait_send())
        pl.when(has_lo)(lambda: dec_dn(b).wait_send())
        ra_up(b).wait_send()
        ra_dn(b).wait_send()
        to_twin(0, b).wait_send()
        to_twin(1, b).wait_send()
        return carry

    lax.fori_loop(0, blocks, finish, 0)
    each_peer(lambda p: reducing(p, lambda: rs(p, rank).wait_send()))
    each_peer(lambda p: au(p, rank).wait_send())
    reducing(rank, lambda: each_peer(lambda p: ag(p, rank).wait_send()))


def per_device(n_ra, n_dec, sky_maps, radii, valid):
    chans, rows, cols = sky_maps.shape
    blocks = chans // CB
    rows8 = up(rows, 16)
    groups = cols // WIDE
    per = -(-rows // groups)
    peers = n_ra * n_dec
    share = chans // min(peers, chans // 8)
    tall = max(per * groups, rows8)
    f32, b16, dma = jnp.float32, jnp.bfloat16, pltpu.SemaphoreType.DMA
    vmem = pl.BlockSpec(memory_space=pltpu.VMEM)
    hbm = pl.BlockSpec(memory_space=pltpu.HBM)
    in_at, in_rows, edge_rows = inner_rows(rows)
    inner, outer = rows - 2 * RMAX, 2 * RMAX
    flat = jnp.transpose(sky_maps, (1, 0, 2))
    packed = pltpu.VMEM((blocks, per, CB, cols), b16)
    edge = pltpu.VMEM((blocks, RMAX, CB, cols), b16)
    smoothed, mean, cov = pl.pallas_call(
        functools.partial(kernel, (n_ra, n_dec, rows, chans, cols)),
        out_shape=(
            jax.ShapeDtypeStruct((rows, chans, cols), b16),
            jax.ShapeDtypeStruct((1, chans), f32),
            jax.ShapeDtypeStruct((2 * chans, chans), f32),
        ),
        in_specs=[pl.BlockSpec(memory_space=pltpu.SMEM), hbm, hbm],
        out_specs=(vmem, vmem, vmem),
        scratch_shapes=[
            pltpu.VMEM((rows, chans, cols), b16),
            pltpu.VMEM((rows, cols), jnp.int32),
            dma((2,)),
            pltpu.VMEM((RMAX + 1, 2 * cols, cols), b16),
            pltpu.VMEM((RMAX + 1, in_rows, 128), b16),
            pltpu.VMEM((RMAX + 1, 2 * edge_rows, 128), b16),
            pltpu.VMEM((tall * CB, cols), f32),
            pltpu.VMEM((tall * CB, cols), f32),
            pltpu.VMEM((rows8 * CB, cols), f32),
            pltpu.VMEM((blocks, 128 * CB, cols), f32),
            pltpu.VMEM((rows, CB, cols), b16),
            pltpu.VMEM((blocks, inner, CB, cols), b16),
            pltpu.VMEM((blocks, outer, CB, cols), b16),
            pltpu.VMEM((blocks, inner, CB, cols), b16),
            pltpu.VMEM((blocks, outer, CB, cols), b16),
            packed, packed, packed, packed,
            edge, edge, edge, edge,
            pltpu.VMEM((chans + CB, 2 * chans), f32),
            pltpu.VMEM((peers, share, 2 * chans), f32),
            pltpu.VMEM((chans, 2 * chans), f32),
            pltpu.VMEM((8, 2 * chans), f32),
            pltpu.VMEM((peers, 8, 2 * chans), f32),
            dma((2, blocks)), dma((2, blocks)), dma((2, blocks)), dma((2, blocks)),
            dma((2, blocks)), dma((2, blocks)),
            dma((peers,)), dma((peers,)), dma((peers,)), dma((peers,)), dma((peers,)), dma((peers,)),
        ],
        compiler_params=pltpu.CompilerParams(
            collective_id=0, has_side_effects=True, vmem_limit_bytes=32 * 1024 * 1024
        ),
    )(radii, flat, valid)
    return (jnp.transpose(smoothed, (1, 0, 2)), mean.reshape(chans), cov)


def solution(mesh):
    return jax.shard_map(
        functools.partial(per_device, mesh.shape["ra"], mesh.shape["dec"]),
        mesh=mesh,
        in_specs=(
            P(("groups", "band"), "ra", "dec"),
            P(("groups", "band")),
            P(("groups", "ra"), "dec"),
        ),
        out_specs=(P(("groups", "band"), "ra", "dec"), P(("groups", "band")), P("groups", "band")),
        check_vma=False,
    )
```
